32 devices in a mesh: layer: 4 (over x, core), sub: 8 (over z, y).
Axes of the slice: x: 2, y: 2, z: 4, core: 2. Of those that a mesh axis runs over, the one named last changes fastest.
Arguments:
- screens: float32 [4, 7, 2048, 640], P('layer', None, None, 'sub'), may hold values from -4 to 4
- new_columns: float32 [10, 4, 2048, 8], P(None, 'layer'), may hold values from -4 to 4
- col_block: int32 [10, 4], P(None, 'layer'), may hold values from 240 to 319
- shift_x: int32 [10, 4, 6], P(None, 'layer'), may hold values from -40 to 40, as said below
- shift_y: int32 [10, 4, 6], P(None, 'layer'), may hold values from -40 to 40, as said below
- valid: int32 [80, 80], P('layer', 'sub'), may hold values 0 or 1
- recon: bfloat16 [6, 2, 80, 80, 5376], P(None, None, 'layer', 'sub'), may hold values from -0.0234375 to 0.0234375
Outputs:
- slopes: float32 [10, 6, 2, 80, 80], P(None, None, None, 'layer', 'sub')
- commands: float32 [10, 5376], replicated
The draws below stay inside these ranges and needn't reach their ends.
Inputs may be any that keep to these rules, and one draw needn't show every extreme that they name: `shift_x`: column shifts reach both -40 and 40 in every draw. `shift_y`: row shifts reach both -40 and 40 in every draw.
All inputs are finite; a program needn't handle non-finite values. No bound on the sum of `valid` on one device may be relied on, other than what follows from the above.
Results may differ from the reference program's by a relative error of at most 0.0029.
Values sent between devices are 32-bit elements; how exact they have to be, the bound alone decides.
A program may use at most 192 MiB of HBM per device.

```python
import math
import jax
import jax.numpy as jnp
from jax import lax

NSUBAP = 80
FFT_LEN = 16
STARS = 6
ACTS = 5376
SCR_ROWS = 2048
TURNS = 7
STEPS = 10
HALO = 40
NEW_COLS = 8
LAYERS = 4
PUP = 640
PUP_TURN = 3
ROW0 = 704


def draw_shift_x(key, part):
    values = jax.random.randint(key, (STEPS, LAYERS, STARS), -HALO, HALO + 1)
    values = values.at[0, 0, 0].set(HALO)
    return values.at[0, 0, 1].set(-HALO)


def draw_shift_y(key, part):
    values = jax.random.randint(jax.random.fold_in(key, 7), (STEPS, LAYERS, STARS), -HALO, HALO + 1)
    values = values.at[0, 1, 2].set(HALO)
    return values.at[0, 1, 3].set(-HALO)


def plant(values, key, least, high):
    longest = values.shape.index(max(values.shape))
    spots = []
    for shift in (0, 1):
        where = [jax.random.randint(jax.random.fold_in(key, axis), (), 0, length) for axis, length in enumerate(values.shape)]
        where[longest] = (where[longest] + shift) % values.shape[longest]
        spots.append(tuple(where))
    return values.at[spots[0]].set(least).at[spots[1]].set(high)


def shard_levels(key, shape, cuts, least, high):
    def one(position, blocks):
        draws = jax.random.uniform(jax.random.fold_in(jax.random.fold_in(key, 6), position), (blocks,), jnp.float32, least / len(cuts), high / len(cuts))
        return jnp.repeat(jnp.exp(draws), shape[position] // blocks).reshape((-1,) + (1,) * (len(shape) - position - 1))

    level = one(*cuts[0])
    for cut in cuts[1:]:
        level = level * one(*cut)
    return level


def gaussian(stream_key, shape, spread, bound, shards=(), kind=jnp.bfloat16):
    gain = shard_levels(stream_key, shape, shards, -0.22, 0.18) if shards else 1.0
    values = jax.random.normal(stream_key, shape, jnp.float32) * spread * gain
    return jnp.minimum(jnp.maximum(values, -bound), bound).astype(kind)


def setup_inputs(seed: int = 0) -> dict:
    seeds = jax.random.split(jax.random.key(seed), 8)
    screens = gaussian(seeds[0], (LAYERS, TURNS, SCR_ROWS, PUP), 0.3, 4.0, ((0, 4), (3, 8)), jnp.float32)
    new_columns = gaussian(seeds[1], (STEPS, LAYERS, SCR_ROWS, NEW_COLS), 0.3, 4.0, ((1, 4),), jnp.float32)
    col_block = plant(jax.random.randint(seeds[2], (STEPS, LAYERS), PUP_TURN * PUP // NEW_COLS, (PUP_TURN + 1) * PUP // NEW_COLS), jax.random.fold_in(seeds[2], 1), PUP_TURN * PUP // NEW_COLS, ((PUP_TURN + 1) * PUP // NEW_COLS) - 1).astype(jnp.int32)
    shift_x = draw_shift_x(jax.random.fold_in(seeds[7], 71), 0)
    shift_y = draw_shift_y(jax.random.fold_in(seeds[7], 71), 0)
    valid = plant((jax.random.randint(seeds[5], (NSUBAP, NSUBAP), 0, 4) < 3).astype(jnp.int32), jax.random.fold_in(seeds[5], 1), 0, 1)
    recon = gaussian(seeds[6], (STARS, 2, NSUBAP, NSUBAP, ACTS), (2 * STARS * NSUBAP * NSUBAP) ** -0.5, 0.0234375, ((2, 4), (3, 8)))
    return {"screens": screens, "new_columns": new_columns, "col_block": col_block, "shift_x": shift_x, "shift_y": shift_y, "valid": valid, "recon": recon}


def lenslet_slopes(phase, valid, fft_len):
    stars, rows, cols = phase.shape
    subs_r, subs_c = valid.shape
    pix = rows // subs_r
    tiles = phase.reshape(stars, subs_r, pix, subs_c, pix)
    tiles = jnp.transpose(tiles, (2, 4, 0, 1, 3)).reshape(pix, pix, stars * subs_r * subs_c)
    freq = jnp.arange(fft_len).astype(jnp.float32)
    place = jnp.arange(pix).astype(jnp.float32)
    angle = (2.0 * math.pi / fft_len) * freq[:, None] * place[None, :]
    cosine = jnp.cos(angle)
    sine = -jnp.sin(angle)
    real_part = jnp.cos(tiles)
    imag_part = jnp.sin(tiles)
    highest = lax.Precision.HIGHEST

    def along_rows(mat, field):
        return jnp.einsum('kn,nms->kms', mat, field, precision=highest)

    def along_cols(field, mat):
        return jnp.einsum('kms,qm->kqs', field, mat, precision=highest)

    first_re = along_rows(cosine, real_part) - along_rows(sine, imag_part)
    first_im = along_rows(cosine, imag_part) + along_rows(sine, real_part)
    spot_re = along_cols(first_re, cosine) - along_cols(first_im, sine)
    spot_im = along_cols(first_re, sine) + along_cols(first_im, cosine)
    power = spot_re * spot_re + spot_im * spot_im
    centred = ((jnp.arange(fft_len) + fft_len // 2) % fft_len - fft_len // 2).astype(jnp.float32)
    total = jnp.sum(power, axis=(0, 1))
    along_x = jnp.sum(power * centred[None, :, None], axis=(0, 1)) / total
    along_y = jnp.sum(power * centred[:, None, None], axis=(0, 1)) / total
    result = jnp.stack([along_x, along_y]).reshape(2, stars, subs_r, subs_c)
    return jnp.transpose(result, (1, 0, 2, 3)) * valid.astype(jnp.float32)[None, None]


def write_columns(screen, fresh, block):
    column = (block * NEW_COLS).astype(jnp.int32)
    turn = (column // PUP).astype(jnp.int32)
    within = (column % PUP).astype(jnp.int32)
    return lax.dynamic_update_slice(screen, fresh[None], (turn, jnp.int32(0), within))


def footprint(screens, step_x, step_y):
    def one_layer(screen, sx, sy):
        band = screen[PUP_TURN - 1:PUP_TURN + 2, ROW0 - HALO:ROW0 + PUP + HALO, :]
        band = jnp.transpose(band, (1, 0, 2)).reshape(PUP + 2 * HALO, 3 * PUP)
        return lax.dynamic_slice(band, ((HALO + sy).astype(jnp.int32), (PUP + sx).astype(jnp.int32)), (PUP, PUP))

    return jnp.sum(jax.vmap(one_layer)(screens, step_x, step_y), axis=0)


def reference(screens, new_columns, col_block, shift_x, shift_y, valid, recon):
    matrix = recon.reshape(-1, ACTS)

    def advance(current, inputs):
        fresh, blocks, step_x, step_y = inputs
        current = jax.vmap(write_columns)(current, fresh, blocks)
        phase = jax.vmap(lambda a, b: footprint(current, a, b), in_axes=(1, 1))(step_x, step_y)
        slopes = lax.map(lambda p: lenslet_slopes(p[None], valid, FFT_LEN)[0], phase)
        flat = slopes.astype(jnp.bfloat16).reshape(-1)
        command = jnp.dot(flat, matrix, preferred_element_type=jnp.float32)
        return current, (slopes, command)

    final, (slopes, commands) = lax.scan(advance, screens, (new_columns, col_block, shift_x, shift_y))
    return slopes, commands
```

```python
import functools
import math

import jax
import jax.numpy as jnp
import numpy as np
from jax import lax
from jax.experimental import pallas as pl
from jax.experimental.pallas import tpu as pltpu
from jax.sharding import PartitionSpec as P

FFT_LEN = 16
ACTS = 5376
HALO = 40
NEW_COLS = 8
PUP = 640
PUP_TURN = 3
ROW0 = 704
PIX = 8
LANES = 128
GROUP = 3
SUBS = 16


def sin_cos(x):
    k = jnp.floor(x * np.float32(2.0 / math.pi) + np.float32(0.5))
    r = x - k * np.float32(1.5703125)
    r = r - k * np.float32(4.837512969970703125e-4)
    r = r - k * np.float32(7.54978995489188216e-8)
    z = r * r
    sr = (np.float32(-1.9515295891e-4) * z + np.float32(8.3321608736e-3)) * z
    sr = r + r * z * (sr + np.float32(-1.6666654611e-1))
    cr = (np.float32(2.443315711809948e-5) * z + np.float32(-1.388731625493765e-3)) * z
    cr = z * z * (cr + np.float32(4.166664568298827e-2))
    cr = cr - np.float32(0.5) * z + np.float32(1.0)
    q = k.astype(jnp.int32)
    swap = (q & 1) == 1
    s = jnp.where(swap, cr, sr)
    c = jnp.where(swap, sr, cr)
    s = jnp.where((q & 2) == 2, -s, s)
    c = jnp.where(((q + 1) & 2) == 2, -c, c)
    return s, c


def split(x):
    high = x.astype(jnp.bfloat16)
    low = (x - high.astype(jnp.float32)).astype(jnp.bfloat16)
    return high, low


def lenslet_constants(cols, used):
    place = np.arange(PIX)
    diff = place[:, None] - place[None, :]
    gap = np.where(diff == 0, 1, np.abs(diff))
    weight = -((-1.0) ** gap) / np.tan(np.pi * gap / FFT_LEN)
    odd = np.where(diff == 0, 0.0, np.sign(diff) * weight)
    sign = (-1.0) ** place
    even = -0.5 * sign[:, None] * sign[None, :]

    def parts(mat):
        high = mat.astype(jnp.bfloat16)
        return high, (mat - high.astype(np.float64)).astype(jnp.bfloat16)

    odd_c = np.kron(np.eye(cols // PIX), odd)
    even_c = np.kron(np.eye(cols // PIX), even).astype(jnp.bfloat16)
    high, low = parts(odd_c)
    zero = np.zeros_like(high)
    left_c = np.concatenate(
        [np.concatenate([high, high, low], 1), np.concatenate([even_c, even_c, zero], 1)], 0
    )
    left_s = np.concatenate([even_c, even_c], 1)
    high, low = parts(np.kron(np.eye(LANES // PIX), odd.T))
    even_r = np.kron(np.eye(LANES // PIX), even).astype(jnp.bfloat16)
    zero = np.zeros_like(high)
    right_c = np.concatenate(
        [np.concatenate([high, low], 1), np.concatenate([high, zero], 1)], 0
    )
    right_e = np.concatenate([even_r, even_r], 0)
    sum_l = np.zeros((SUBS, cols))
    for c in range(used):
        sum_l[c // PIX, c] = 1.0
    sum_l = np.concatenate([sum_l, sum_l], 1).astype(jnp.bfloat16)
    sum_r = np.zeros((LANES, LANES))
    for c in range(LANES):
        sum_r[c, c // PIX] = 1.0
    sum_r = np.concatenate([sum_r, sum_r], 0).astype(jnp.bfloat16)
    return [jnp.asarray(m) for m in (left_c, left_s, right_c, right_e, sum_l, sum_r)]


def mm(a, b):
    return jnp.dot(a, b, preferred_element_type=jnp.float32)


def lenslet_kernel(
    layers, stars, rows, cols, ext,
    blk_ref, sx_ref, sy_ref, band_ref,
    left_c_ref, left_s_ref, right_c_ref, right_e_ref, sum_l_ref, sum_r_ref,
    out_ref, screen_ref,
):
    main = rows // LANES
    rem = rows % LANES
    tiles = band_ref.shape[2] // LANES
    groups = stars // GROUP
    lane = lax.broadcasted_iota(jnp.int32, (cols, LANES), 1)

    for l in range(layers):
        for j in range(tiles):
            screen_ref[l, j, 0:ext, :] = band_ref[l, 0:ext, j * LANES : (j + 1) * LANES]

    def body(i, carry):
        t = i // groups
        h = i % groups
        for l in range(layers):
            start = pl.multiple_of(blk_ref[t * layers + l] * NEW_COLS, NEW_COLS)
            row = pl.multiple_of(ext + t * NEW_COLS, NEW_COLS)
            for j in range(tiles):
                screen_ref[l, j, pl.ds(start, NEW_COLS), :] = band_ref[
                    l, pl.ds(row, NEW_COLS), j * LANES : (j + 1) * LANES
                ]
        parts = []
        tail = None
        for k in range(GROUP):
            sums = [None] * (main + 1)
            for l in range(layers):
                at = (t * layers + l) * stars + h * GROUP + k
                dx = sx_ref[at] + HALO
                dy = sy_ref[at] + HALO
                turn = lax.rem(LANES - dy, LANES)
                rolled = [
                    pltpu.roll(screen_ref[l, j, pl.ds(dx, cols), :], turn, 1)
                    for j in range(main + 1)
                ]
                keep = lane < LANES - dy
                for j in range(main + 1):
                    if j < main:
                        piece = jnp.where(keep, rolled[j], rolled[j + 1])
                    else:
                        piece = rolled[j]
                    sums[j] = piece if sums[j] is None else sums[j] + piece
            parts.extend(sums[:main])
            if rem:
                moved = sums[main] if k == 0 else pltpu.roll(sums[main], k * rem, 1)
                tail = moved if tail is None else jnp.where(lane < k * rem, tail, moved)
        if rem:
            parts.append(tail)
        phase = jnp.concatenate(parts, axis=1)
        s, c = sin_cos(phase)
        ch, cl = split(c)
        sh, sl = split(s)
        from_c = mm(left_c_ref[...], jnp.concatenate([ch, cl, ch], axis=0))
        from_s = mm(left_s_ref[...], jnp.concatenate([sh, sl], axis=0))
        along_x = s * (from_c[0:cols] + from_s) + c * from_c[cols:]
        power = c * c + s * s
        along_y = []
        for j in range(len(parts)):
            cut = slice(j * LANES, (j + 1) * LANES)
            pair_c = jnp.concatenate([ch[:, cut], cl[:, cut]], axis=1)
            pair_s = jnp.concatenate([sh[:, cut], sl[:, cut]], axis=1)
            odd = mm(pair_c, right_c_ref[...])
            odd = odd[:, :LANES] + odd[:, LANES:]
            along_y.append(
                s[:, cut] * (odd + mm(pair_s, right_e_ref[...]))
                + c[:, cut] * mm(pair_c, right_e_ref[...])
            )
        every = jnp.concatenate([along_x] + along_y + [power], axis=1)
        high, low = split(every)
        every = mm(sum_l_ref[...], jnp.concatenate([high, low], axis=0))
        count = 3 * len(parts)
        every = jnp.concatenate(
            [every[:, j * LANES : (j + 1) * LANES] for j in range(count)], axis=0
        )
        high, low = split(every)
        every = mm(jnp.concatenate([high, low], axis=1), sum_r_ref[...])
        size = len(parts) * SUBS
        total = every[2 * size :]
        out_ref[i, 0] = every[:size] / total
        out_ref[i, 1] = every[size : 2 * size] / total
        return carry

    lax.fori_loop(0, blk_ref.shape[0] // layers * groups, body, 0)


def lenslet_slopes(band, blocks, step_x, step_y, rows, cols, ext, interpret=False):
    steps, layers, stars = step_x.shape
    padded = ext - 2 * HALO
    main = rows // LANES
    tiles = GROUP * main + (1 if rows % LANES else 0)
    groups = stars // GROUP
    smem = pl.BlockSpec(memory_space=pltpu.SMEM)
    vmem = pl.BlockSpec(memory_space=pltpu.VMEM)
    out = pl.pallas_call(
        functools.partial(lenslet_kernel, layers, stars, rows, padded, ext),
        out_shape=jax.ShapeDtypeStruct((steps * groups, 2, tiles * SUBS, LANES), jnp.float32),
        in_specs=[smem] * 3 + [vmem] * 7,
        out_specs=vmem,
        scratch_shapes=[
            pltpu.VMEM((layers, band.shape[2] // LANES, ext + NEW_COLS, LANES), jnp.float32)
        ],
        compiler_params=pltpu.CompilerParams(vmem_limit_bytes=40 * 1024 * 1024),
        interpret=interpret,
    )(
        blocks.reshape(-1), step_x.reshape(-1), step_y.reshape(-1), band,
        *lenslet_constants(padded, cols),
    )
    out = out.reshape(steps, groups, 2, tiles, SUBS, LANES)[:, :, :, :, : cols // PIX]
    found = []
    if main:
        part = out[:, :, :, : GROUP * main, :, : LANES // PIX]
        part = part.reshape(steps, groups, 2, GROUP, main, cols // PIX, LANES // PIX)
        part = jnp.transpose(part, (0, 1, 3, 5, 2, 4, 6))
        found.append(part.reshape(steps, stars, cols // PIX, 2, main * LANES // PIX))
    rem = rows % LANES // PIX
    if rem:
        part = out[:, :, :, GROUP * main, :, : GROUP * rem]
        part = part.reshape(steps, groups, 2, cols // PIX, GROUP, rem)
        part = jnp.transpose(part, (0, 1, 4, 3, 2, 5))
        found.append(part.reshape(steps, stars, cols // PIX, 2, rem))
    return jnp.concatenate(found, axis=4) if len(found) > 1 else found[0]


def local(screens, new_columns, col_block, shift_x, shift_y, valid, recon):
    width = screens.shape[3]
    steps, _, stars = shift_x.shape
    count = lax.axis_size("layer")
    owner = lax.axis_index("sub")
    subs = lax.axis_size("sub")
    rows = valid.shape[0] * PIX
    cols = -(-width // 16) * 16
    ext = cols + 2 * HALO
    lanes = -(-(rows + 2 * HALO) // LANES) * LANES

    band = screens[0, PUP_TURN - 1 : PUP_TURN + 2, ROW0 - HALO : ROW0 + PUP + HALO, :]
    band = jnp.transpose(band, (0, 2, 1))
    tail = jnp.where(owner == subs - 1, band[0, width - HALO :], band[1, width - HALO :])
    head = jnp.where(owner == 0, band[2, :HALO], band[1, :HALO])
    forward = [(i, (i + 1) % subs) for i in range(subs)]
    backward = [(b, a) for a, b in forward]
    before = lax.ppermute(tail, "sub", forward)
    after = lax.ppermute(head, "sub", backward)
    fresh = jnp.transpose(new_columns[:, 0, ROW0 - HALO : ROW0 + PUP + HALO, :], (0, 2, 1))
    fresh = fresh.reshape(steps * NEW_COLS, PUP + 2 * HALO)
    pieces = [before, band[1], after]
    if cols > width:
        pieces.append(jnp.zeros((cols - width, PUP + 2 * HALO), jnp.float32))
    strip = jnp.concatenate(pieces + [fresh], axis=0)
    plan = jnp.concatenate(
        [col_block.reshape(-1), shift_x.reshape(-1), shift_y.reshape(-1)]
    ).astype(jnp.float32)
    lines = -(-plan.shape[0] // lanes)
    plan = jnp.pad(plan, (0, 8 * lanes - plan.shape[0])).reshape(8, lanes)

    def share(i):
        cut = strip[:, i * rows : i * rows + rows + 2 * HALO]
        cut = jnp.pad(cut, ((0, 0), (0, lanes - cut.shape[1])))
        return jnp.concatenate([cut, plan], axis=0)

    sent = jnp.stack([share(i) for i in range(count)])
    got = lax.all_to_all(sent, "layer", split_axis=0, concat_axis=0, tiled=True)

    last = ext + steps * NEW_COLS
    plans = got[:, last : last + lines].reshape(count, -1).astype(jnp.int32)
    blocks = plans[:, :steps].T
    step_x = plans[:, steps : steps + steps * stars].reshape(count, steps, stars)
    step_y = plans[:, steps + steps * stars : steps + 2 * steps * stars]
    step_x = jnp.transpose(step_x, (1, 0, 2))
    step_y = jnp.transpose(step_y.reshape(count, steps, stars), (1, 0, 2))
    spot = blocks - PUP_TURN * PUP // NEW_COLS - owner * (width // NEW_COLS) + HALO // NEW_COLS
    inside = (spot >= 0) & (spot < (width + 2 * HALO) // NEW_COLS)
    spot = jnp.where(inside, spot, ext // NEW_COLS)

    slopes = lenslet_slopes(got, spot, step_x, step_y, rows, width, ext)
    slopes = slopes * valid.T.astype(jnp.float32)[None, None, :, None, :]
    flat = jnp.transpose(slopes, (0, 1, 4, 2, 3)).astype(jnp.bfloat16).reshape(steps, -1)
    matrix = jnp.transpose(recon, (0, 2, 3, 1, 4)).reshape(-1, ACTS)
    part = jnp.dot(flat, matrix, preferred_element_type=jnp.float32)
    commands = lax.psum(part, ("layer", "sub"))
    return (jnp.transpose(slopes, (0, 1, 3, 4, 2)), commands)


def solution(mesh):
    return jax.shard_map(
        local,
        mesh=mesh,
        in_specs=(
            P("layer", None, None, "sub"),
            P(None, "layer", None, None),
            P(None, "layer"),
            P(None, "layer", None),
            P(None, "layer", None),
            P("layer", "sub"),
            P(None, None, "layer", "sub", None),
        ),
        out_specs=(P(None, None, None, "layer", "sub"), P()),
        check_vma=False,
    )
```

```python
import functools
import math

import jax
import jax.numpy as jnp
import numpy as np
from jax import lax
from jax.experimental import pallas as pl
from jax.experimental.pallas import tpu as pltpu
from jax.sharding import PartitionSpec as P

FFT_LEN = 16
ACTS = 5376
HALO = 40
NEW_COLS = 8
PUP = 640
PUP_TURN = 3
ROW0 = 704
PIX = 8
LANES = 128
GROUP = 3
SUBS = 16


def sin_cos(x):
    k = jnp.floor(x * np.float32(2.0 / math.pi) + np.float32(0.5))
    r = x - k * np.float32(1.5703125)
    r = r - k * np.float32(4.837512969970703125e-4)
    r = r - k * np.float32(7.54978995489188216e-8)
    z = r * r
    sr = (np.float32(-1.9515295891e-4) * z + np.float32(8.3321608736e-3)) * z
    sr = r + r * z * (sr + np.float32(-1.6666654611e-1))
    cr = (np.float32(2.443315711809948e-5) * z + np.float32(-1.388731625493765e-3)) * z
    cr = z * z * (cr + np.float32(4.166664568298827e-2))
    cr = cr - np.float32(0.5) * z + np.float32(1.0)
    q = k.astype(jnp.int32)
    swap = (q & 1) == 1
    s = jnp.where(swap, cr, sr)
    c = jnp.where(swap, sr, cr)
    s = jnp.where((q & 2) == 2, -s, s)
    c = jnp.where(((q + 1) & 2) == 2, -c, c)
    return s, c


def split(x):
    high = x.astype(jnp.bfloat16)
    low = (x - high.astype(jnp.float32)).astype(jnp.bfloat16)
    return high, low


def lenslet_constants(cols, used):
    place = np.arange(PIX)
    diff = place[:, None] - place[None, :]
    gap = np.where(diff == 0, 1, np.abs(diff))
    weight = -((-1.0) ** gap) / np.tan(np.pi * gap / FFT_LEN)
    odd = np.where(diff == 0, 0.0, np.sign(diff) * weight)
    sign = (-1.0) ** place
    even = -0.5 * sign[:, None] * sign[None, :]

    def parts(mat):
        high = mat.astype(jnp.bfloat16)
        return high, (mat - high.astype(np.float64)).astype(jnp.bfloat16)

    odd_c = np.kron(np.eye(cols // PIX), odd)
    even_c = np.kron(np.eye(cols // PIX), even).astype(jnp.bfloat16)
    high, low = parts(odd_c)
    zero = np.zeros_like(high)
    left_c = np.concatenate(
        [np.concatenate([high, high, low], 1), np.concatenate([even_c, even_c, zero], 1)], 0
    )
    left_s = np.concatenate([even_c, even_c], 1)
    high, low = parts(np.kron(np.eye(LANES // PIX), odd.T))
    even_r = np.kron(np.eye(LANES // PIX), even).astype(jnp.bfloat16)
    zero = np.zeros_like(high)
    right_c = np.concatenate(
        [np.concatenate([high, low], 1), np.concatenate([high, zero], 1)], 0
    )
    right_e = np.concatenate([even_r, even_r], 0)
    sum_l = np.zeros((SUBS, cols))
    for c in range(used):
        sum_l[c // PIX, c] = 1.0
    sum_l = np.concatenate([sum_l, sum_l], 1).astype(jnp.bfloat16)
    sum_r = np.zeros((LANES, LANES))
    for c in range(LANES):
        sum_r[c, c // PIX] = 1.0
    sum_r = np.concatenate([sum_r, sum_r], 0).astype(jnp.bfloat16)
    return [jnp.asarray(m) for m in (left_c, left_s, right_c, right_e, sum_l, sum_r)]


def mm(a, b):
    return jnp.dot(a, b, preferred_element_type=jnp.float32)


def lenslet_kernel(
    layers, stars, rows, cols, ext,
    blk_ref, sx_ref, sy_ref, band_ref,
    left_c_ref, left_s_ref, right_c_ref, right_e_ref, sum_l_ref, sum_r_ref,
    out_ref, screen_ref,
):
    main = rows // LANES
    rem = rows % LANES
    tiles = band_ref.shape[2] // LANES
    groups = stars // GROUP
    lane = lax.broadcasted_iota(jnp.int32, (cols, LANES), 1)

    for l in range(layers):
        for j in range(tiles):
            screen_ref[l, j, 0:ext, :] = band_ref[l, 0:ext, j * LANES : (j + 1) * LANES]

    def body(i, carry):
        t = i // groups
        h = i % groups
        for l in range(layers):
            start = pl.multiple_of(blk_ref[t * layers + l] * NEW_COLS, NEW_COLS)
            row = pl.multiple_of(ext + t * NEW_COLS, NEW_COLS)
            for j in range(tiles):
                screen_ref[l, j, pl.ds(start, NEW_COLS), :] = band_ref[
                    l, pl.ds(row, NEW_COLS), j * LANES : (j + 1) * LANES
                ]
        parts = []
        tail = None
        for k in range(GROUP):
            sums = [None] * (main + 1)
            for l in range(layers):
                at = (t * layers + l) * stars + h * GROUP + k
                dx = sx_ref[at] + HALO
                dy = sy_ref[at] + HALO
                turn = lax.rem(LANES - dy, LANES)
                rolled = [
                    pltpu.roll(screen_ref[l, j, pl.ds(dx, cols), :], turn, 1)
                    for j in range(main + 1)
                ]
                keep = lane < LANES - dy
                for j in range(main + 1):
                    if j < main:
                        piece = jnp.where(keep, rolled[j], rolled[j + 1])
                    else:
                        piece = rolled[j]
                    sums[j] = piece if sums[j] is None else sums[j] + piece
            parts.extend(sums[:main])
            if rem:
                moved = sums[main] if k == 0 else pltpu.roll(sums[main], k * rem, 1)
                tail = moved if tail is None else jnp.where(lane < k * rem, tail, moved)
        if rem:
            parts.append(tail)
        phase = jnp.concatenate(parts, axis=1)
        s, c = sin_cos(phase)
        ch, cl = split(c)
        sh, sl = split(s)
        from_c = mm(left_c_ref[...], jnp.concatenate([ch, cl, ch], axis=0))
        from_s = mm(left_s_ref[...], jnp.concatenate([sh, sl], axis=0))
        along_x = s * (from_c[0:cols] + from_s) + c * from_c[cols:]
        power = c * c + s * s
        along_y = []
        for j in range(len(parts)):
            cut = slice(j * LANES, (j + 1) * LANES)
            pair_c = jnp.concatenate([ch[:, cut], cl[:, cut]], axis=1)
            pair_s = jnp.concatenate([sh[:, cut], sl[:, cut]], axis=1)
            odd = mm(pair_c, right_c_ref[...])
            odd = odd[:, :LANES] + odd[:, LANES:]
            along_y.append(
                s[:, cut] * (odd + mm(pair_s, right_e_ref[...]))
                + c[:, cut] * mm(pair_c, right_e_ref[...])
            )
        every = jnp.concatenate([along_x] + along_y + [power], axis=1)
        high, low = split(every)
        every = mm(sum_l_ref[...], jnp.concatenate([high, low], axis=0))
        count = 3 * len(parts)
        every = jnp.concatenate(
            [every[:, j * LANES : (j + 1) * LANES] for j in range(count)], axis=0
        )
        high, low = split(every)
        every = mm(jnp.concatenate([high, low], axis=1), sum_r_ref[...])
        size = len(parts) * SUBS
        total = every[2 * size :]
        out_ref[i, 0] = every[:size] / total
        out_ref[i, 1] = every[size : 2 * size] / total
        return carry

    lax.fori_loop(0, blk_ref.shape[0] // layers * groups, body, 0)


def lenslet_slopes(band, blocks, step_x, step_y, rows, cols, ext, interpret=False):
    steps, layers, stars = step_x.shape
    padded = ext - 2 * HALO
    main = rows // LANES
    tiles = GROUP * main + (1 if rows % LANES else 0)
    groups = stars // GROUP
    smem = pl.BlockSpec(memory_space=pltpu.SMEM)
    vmem = pl.BlockSpec(memory_space=pltpu.VMEM)
    out = pl.pallas_call(
        functools.partial(lenslet_kernel, layers, stars, rows, padded, ext),
        out_shape=jax.ShapeDtypeStruct((steps * groups, 2, tiles * SUBS, LANES), jnp.float32),
        in_specs=[smem] * 3 + [vmem] * 7,
        out_specs=vmem,
        scratch_shapes=[
            pltpu.VMEM((layers, band.shape[2] // LANES, ext + NEW_COLS, LANES), jnp.float32)
        ],
        compiler_params=pltpu.CompilerParams(vmem_limit_bytes=40 * 1024 * 1024),
        interpret=interpret,
    )(
        blocks.reshape(-1), step_x.reshape(-1), step_y.reshape(-1), band,
        *lenslet_constants(padded, cols),
    )
    out = out.reshape(steps, groups, 2, tiles, SUBS, LANES)[:, :, :, :, : cols // PIX]
    found = []
    if main:
        part = out[:, :, :, : GROUP * main, :, : LANES // PIX]
        part = part.reshape(steps, groups, 2, GROUP, main, cols // PIX, LANES // PIX)
        part = jnp.transpose(part, (0, 1, 3, 5, 2, 4, 6))
        found.append(part.reshape(steps, stars, cols // PIX, 2, main * LANES // PIX))
    rem = rows % LANES // PIX
    if rem:
        part = out[:, :, :, GROUP * main, :, : GROUP * rem]
        part = part.reshape(steps, groups, 2, cols // PIX, GROUP, rem)
        part = jnp.transpose(part, (0, 1, 4, 3, 2, 5))
        found.append(part.reshape(steps, stars, cols // PIX, 2, rem))
    return jnp.concatenate(found, axis=4) if len(found) > 1 else found[0]


def sum_kernel(
    part_ref, out_ref, by_layer, by_sub, mine,
    send_1, recv_1, send_2, recv_2, send_3, recv_3, send_4, recv_4,
):
    layers, subs = part_ref.shape[0], part_ref.shape[1]
    me_l = lax.axis_index("layer")
    me_s = lax.axis_index("sub")
    mesh_id = pl.DeviceIdType.MESH
    layer_peers = [lax.rem(me_l + j, layers) for j in range(1, layers)]
    sub_peers = [lax.rem(me_s + j, subs) for j in range(1, subs)]

    barrier = pltpu.get_barrier_semaphore()
    for p in layer_peers:
        pl.semaphore_signal(barrier, inc=1, device_id=(p, me_s), device_id_type=mesh_id)
    for q in sub_peers:
        pl.semaphore_signal(barrier, inc=1, device_id=(me_l, q), device_id_type=mesh_id)
    pl.semaphore_wait(barrier, layers + subs - 2)

    def push(src, dst, send, recv, j, target):
        copy = pltpu.make_async_remote_copy(
            src_ref=src, dst_ref=dst, send_sem=send.at[j], recv_sem=recv.at[j],
            device_id=target, device_id_type=mesh_id,
        )
        copy.start()
        return copy

    copies = [
        push(part_ref.at[p], by_layer.at[j], send_1, recv_1, j, (p, me_s))
        for j, p in enumerate(layer_peers)
    ]
    for copy in copies:
        copy.wait()
    total = part_ref[me_l]
    for j in range(layers - 1):
        total = total + by_layer[j]
    mine[...] = total

    copies = [
        push(mine.at[q], by_sub.at[j], send_2, recv_2, j, (me_l, q))
        for j, q in enumerate(sub_peers)
    ]
    for copy in copies:
        copy.wait()
    total = mine[me_s]
    for j in range(subs - 1):
        total = total + by_sub[j]
    out_ref[me_l, me_s] = total

    own = out_ref.at[me_l, me_s]
    copies = [
        push(own, own, send_3, recv_3, j, (me_l, q)) for j, q in enumerate(sub_peers)
    ]
    for copy in copies:
        copy.wait()
    own = out_ref.at[me_l]
    copies = [
        push(own, own, send_4, recv_4, j, (p, me_s)) for j, p in enumerate(layer_peers)
    ]
    for copy in copies:
        copy.wait()


def summed_everywhere(part):
    layers = lax.axis_size("layer")
    subs = lax.axis_size("sub")
    lines = part.size // LANES
    chunk = -(-lines // (layers * subs * 8)) * 8
    padded = jnp.pad(part.reshape(lines, LANES), ((0, layers * subs * chunk - lines), (0, 0)))
    padded = padded.reshape(layers, subs, chunk, LANES)
    vmem = pl.BlockSpec(memory_space=pltpu.VMEM)
    dma = pltpu.SemaphoreType.DMA
    total = pl.pallas_call(
        sum_kernel,
        out_shape=jax.ShapeDtypeStruct(padded.shape, jnp.float32),
        in_specs=[vmem],
        out_specs=vmem,
        scratch_shapes=[
            pltpu.VMEM((layers - 1, subs, chunk, LANES), jnp.float32),
            pltpu.VMEM((subs - 1, chunk, LANES), jnp.float32),
            pltpu.VMEM((subs, chunk, LANES), jnp.float32),
            dma((layers - 1,)), dma((layers - 1,)),
            dma((subs - 1,)), dma((subs - 1,)),
            dma((subs - 1,)), dma((subs - 1,)),
            dma((layers - 1,)), dma((layers - 1,)),
        ],
        compiler_params=pltpu.CompilerParams(
            collective_id=0, has_side_effects=True, vmem_limit_bytes=32 * 1024 * 1024
        ),
    )(padded)
    return total.reshape(-1, LANES)[:lines].reshape(part.shape)


def local(screens, new_columns, col_block, shift_x, shift_y, valid, recon):
    width = screens.shape[3]
    steps, _, stars = shift_x.shape
    count = lax.axis_size("layer")
    owner = lax.axis_index("sub")
    subs = lax.axis_size("sub")
    rows = valid.shape[0] * PIX
    cols = -(-width // 16) * 16
    ext = cols + 2 * HALO
    lanes = -(-(rows + 2 * HALO) // LANES) * LANES

    band = screens[0, PUP_TURN - 1 : PUP_TURN + 2, ROW0 - HALO : ROW0 + PUP + HALO, :]
    band = jnp.transpose(band, (0, 2, 1))
    tail = jnp.where(owner == subs - 1, band[0, width - HALO :], band[1, width - HALO :])
    head = jnp.where(owner == 0, band[2, :HALO], band[1, :HALO])
    forward = [(i, (i + 1) % subs) for i in range(subs)]
    backward = [(b, a) for a, b in forward]
    before = lax.ppermute(tail, "sub", forward)
    after = lax.ppermute(head, "sub", backward)
    fresh = jnp.transpose(new_columns[:, 0, ROW0 - HALO : ROW0 + PUP + HALO, :], (0, 2, 1))
    fresh = fresh.reshape(steps * NEW_COLS, PUP + 2 * HALO)
    pieces = [before, band[1], after]
    if cols > width:
        pieces.append(jnp.zeros((cols - width, PUP + 2 * HALO), jnp.float32))
    strip = jnp.concatenate(pieces + [fresh], axis=0)
    plan = jnp.concatenate(
        [col_block.reshape(-1), shift_x.reshape(-1), shift_y.reshape(-1)]
    ).astype(jnp.float32)
    lines = -(-plan.shape[0] // lanes)
    plan = jnp.pad(plan, (0, 8 * lanes - plan.shape[0])).reshape(8, lanes)

    def share(i):
        cut = strip[:, i * rows : i * rows + rows + 2 * HALO]
        cut = jnp.pad(cut, ((0, 0), (0, lanes - cut.shape[1])))
        return jnp.concatenate([cut, plan], axis=0)

    sent = jnp.stack([share(i) for i in range(count)])
    got = lax.all_to_all(sent, "layer", split_axis=0, concat_axis=0, tiled=True)

    last = ext + steps * NEW_COLS
    plans = got[:, last : last + lines].reshape(count, -1).astype(jnp.int32)
    blocks = plans[:, :steps].T
    step_x = plans[:, steps : steps + steps * stars].reshape(count, steps, stars)
    step_y = plans[:, steps + steps * stars : steps + 2 * steps * stars]
    step_x = jnp.transpose(step_x, (1, 0, 2))
    step_y = jnp.transpose(step_y.reshape(count, steps, stars), (1, 0, 2))
    spot = blocks - PUP_TURN * PUP // NEW_COLS - owner * (width // NEW_COLS) + HALO // NEW_COLS
    inside = (spot >= 0) & (spot < (width + 2 * HALO) // NEW_COLS)
    spot = jnp.where(inside, spot, ext // NEW_COLS)

    slopes = lenslet_slopes(got, spot, step_x, step_y, rows, width, ext)
    slopes = slopes * valid.T.astype(jnp.float32)[None, None, :, None, :]
    flat = jnp.transpose(slopes, (0, 1, 4, 2, 3)).astype(jnp.bfloat16).reshape(steps, -1)
    matrix = jnp.transpose(recon, (0, 2, 3, 1, 4)).reshape(-1, ACTS)
    part = jnp.dot(flat, matrix, preferred_element_type=jnp.float32)
    commands = summed_everywhere(part)
    return (jnp.transpose(slopes, (0, 1, 3, 4, 2)), commands)


def solution(mesh):
    return jax.shard_map(
        local,
        mesh=mesh,
        in_specs=(
            P("layer", None, None, "sub"),
            P(None, "layer", None, None),
            P(None, "layer"),
            P(None, "layer", None),
            P(None, "layer", None),
            P("layer", "sub"),
            P(None, None, "layer", "sub", None),
        ),
        out_specs=(P(None, None, None, "layer", "sub"), P()),
        check_vma=False,
    )
```

```python
import functools
import math

import jax
import jax.numpy as jnp
import numpy as np
from jax import lax
from jax.experimental import pallas as pl
from jax.experimental.pallas import tpu as pltpu
from jax.sharding import PartitionSpec as P

FFT_LEN = 16
ACTS = 5376
HALO = 40
NEW_COLS = 8
PUP = 640
PUP_TURN = 3
ROW0 = 704
PIX = 8
LANES = 128
GROUP = 3
SUBS = 16


def sin_cos(x):
    k = jnp.floor(x * np.float32(2.0 / math.pi) + np.float32(0.5))
    r = x - k * np.float32(1.5703125)
    r = r - k * np.float32(4.837512969970703125e-4)
    r = r - k * np.float32(7.54978995489188216e-8)
    z = r * r
    sr = (np.float32(-1.9515295891e-4) * z + np.float32(8.3321608736e-3)) * z
    sr = r + r * z * (sr + np.float32(-1.6666654611e-1))
    cr = (np.float32(2.443315711809948e-5) * z + np.float32(-1.388731625493765e-3)) * z
    cr = z * z * (cr + np.float32(4.166664568298827e-2))
    cr = cr - np.float32(0.5) * z + np.float32(1.0)
    q = k.astype(jnp.int32)
    swap = (q & 1) == 1
    s = jnp.where(swap, cr, sr)
    c = jnp.where(swap, sr, cr)
    s = jnp.where((q & 2) == 2, -s, s)
    c = jnp.where(((q + 1) & 2) == 2, -c, c)
    return s, c


def split(x):
    high = x.astype(jnp.bfloat16)
    low = (x - high.astype(jnp.float32)).astype(jnp.bfloat16)
    return high, low


def lattice(shape):
    return tuple(lax.broadcasted_iota(jnp.int32, shape, axis) for axis in (0, 1))


def odd_form(row, col):
    gap = row - col
    value = jnp.zeros(row.shape, jnp.float32)
    for d in range(1, PIX):
        weight = np.float32(-((-1.0) ** d) / math.tan(math.pi * d / FFT_LEN))
        value = jnp.where(gap == d, weight, jnp.where(gap == -d, -weight, value))
    return jnp.where((row >> 3) == (col >> 3), value, 0.0)


def even_form(row, col):
    value = jnp.where(((row + col) & 1) == 1, np.float32(0.5), np.float32(-0.5))
    return jnp.where((row >> 3) == (col >> 3), value, 0.0)


def fill_constants(cols, used, left_c, left_s, right_c, right_e, sum_l, sum_r):
    row, col = lattice((cols, 3 * cols))
    third = col >= 2 * cols
    inner = col - jnp.where(third, 2 * cols, jnp.where(col >= cols, cols, 0))
    value = odd_form(row, inner)
    high = value.astype(jnp.bfloat16).astype(jnp.float32)
    left_c[0:cols, :] = jnp.where(third, value - high, high).astype(jnp.bfloat16)
    left_c[cols:, :] = jnp.where(third, 0.0, even_form(row, inner)).astype(jnp.bfloat16)
    row, col = lattice((cols, 2 * cols))
    inner = col - jnp.where(col >= cols, cols, 0)
    left_s[...] = even_form(row, inner).astype(jnp.bfloat16)
    row, col = lattice((2 * LANES, 2 * LANES))
    value = odd_form(col & (LANES - 1), row & (LANES - 1))
    high = value.astype(jnp.bfloat16).astype(jnp.float32)
    low = jnp.where(row < LANES, value - high, 0.0)
    right_c[...] = jnp.where(col < LANES, high, low).astype(jnp.bfloat16)
    row, col = lattice((2 * LANES, LANES))
    row = row & (LANES - 1)
    right_e[...] = even_form(row, col).astype(jnp.bfloat16)
    sum_r[...] = jnp.where((row >> 3) == col, 1.0, 0.0).astype(jnp.bfloat16)
    row, col = lattice((SUBS, 2 * cols))
    inner = col - jnp.where(col >= cols, cols, 0)
    inside = ((inner >> 3) == row) & (inner < used)
    sum_l[...] = jnp.where(inside, 1.0, 0.0).astype(jnp.bfloat16)


def mm(a, b):
    return jnp.dot(a, b, preferred_element_type=jnp.float32)


def lenslet_kernel(
    layers, stars, rows, cols, used,
    blk_ref, sx_ref, sy_ref, band_ref, out_ref, screen_ref,
    left_c_ref, left_s_ref, right_c_ref, right_e_ref, sum_l_ref, sum_r_ref,
):
    main = rows // LANES
    rem = rows % LANES
    tiles = band_ref.shape[2] // LANES
    groups = stars // GROUP
    lane = lax.broadcasted_iota(jnp.int32, (cols, LANES), 1)

    fill_constants(
        cols, used, left_c_ref, left_s_ref, right_c_ref, right_e_ref, sum_l_ref, sum_r_ref
    )
    rims = band_ref.shape[1] - 2 * HALO
    for l in range(layers):
        for j in range(tiles):
            cut = slice(j * LANES, (j + 1) * LANES)
            screen_ref[l, j, 0:HALO, :] = band_ref[l, rims : rims + HALO, cut]
            screen_ref[l, j, HALO : HALO + used, :] = band_ref[l, 0:used, cut]
            screen_ref[l, j, HALO + used : 2 * HALO + used, :] = band_ref[l, rims + HALO :, cut]
            if cols > used:
                screen_ref[l, j, 2 * HALO + used : 2 * HALO + cols, :] = jnp.zeros(
                    (cols - used, LANES), jnp.float32
                )

    def body(i, carry):
        t = i // groups
        h = i % groups
        for l in range(layers):
            start = pl.multiple_of(blk_ref[t * layers + l] * NEW_COLS, NEW_COLS)
            row = pl.multiple_of(used + t * NEW_COLS, NEW_COLS)
            for j in range(tiles):
                screen_ref[l, j, pl.ds(start, NEW_COLS), :] = band_ref[
                    l, pl.ds(row, NEW_COLS), j * LANES : (j + 1) * LANES
                ]
        parts = []
        tail = None
        for k in range(GROUP):
            sums = [None] * (main + 1)
            for l in range(layers):
                at = (t * layers + l) * stars + h * GROUP + k
                dx = sx_ref[at] + HALO
                dy = sy_ref[at] + HALO
                turn = lax.rem(LANES - dy, LANES)
                rolled = [
                    pltpu.roll(screen_ref[l, j, pl.ds(dx, cols), :], turn, 1)
                    for j in range(main + 1)
                ]
                keep = lane < LANES - dy
                for j in range(main + 1):
                    if j < main:
                        piece = jnp.where(keep, rolled[j], rolled[j + 1])
                    else:
                        piece = rolled[j]
                    sums[j] = piece if sums[j] is None else sums[j] + piece
            parts.extend(sums[:main])
            if rem:
                moved = sums[main] if k == 0 else pltpu.roll(sums[main], k * rem, 1)
                tail = moved if tail is None else jnp.where(lane < k * rem, tail, moved)
        if rem:
            parts.append(tail)
        phase = jnp.concatenate(parts, axis=1)
        s, c = sin_cos(phase)
        ch, cl = split(c)
        sh, sl = split(s)
        from_c = mm(left_c_ref[...], jnp.concatenate([ch, cl, ch], axis=0))
        from_s = mm(left_s_ref[...], jnp.concatenate([sh, sl], axis=0))
        along_x = s * (from_c[0:cols] + from_s) + c * from_c[cols:]
        power = c * c + s * s
        along_y = []
        for j in range(len(parts)):
            cut = slice(j * LANES, (j + 1) * LANES)
            pair_c = jnp.concatenate([ch[:, cut], cl[:, cut]], axis=1)
            pair_s = jnp.concatenate([sh[:, cut], sl[:, cut]], axis=1)
            odd = mm(pair_c, right_c_ref[...])
            odd = odd[:, :LANES] + odd[:, LANES:]
            along_y.append(
                s[:, cut] * (odd + mm(pair_s, right_e_ref[...]))
                + c[:, cut] * mm(pair_c, right_e_ref[...])
            )
        every = jnp.concatenate([along_x] + along_y + [power], axis=1)
        high, low = split(every)
        every = mm(sum_l_ref[...], jnp.concatenate([high, low], axis=0))
        count = 3 * len(parts)
        every = jnp.concatenate(
            [every[:, j * LANES : (j + 1) * LANES] for j in range(count)], axis=0
        )
        high, low = split(every)
        every = mm(jnp.concatenate([high, low], axis=1), sum_r_ref[...])
        size = len(parts) * SUBS
        total = every[2 * size :]
        out_ref[i, 0] = every[:size] / total
        out_ref[i, 1] = every[size : 2 * size] / total
        return carry

    lax.fori_loop(0, blk_ref.shape[0] // layers * groups, body, 0, unroll=2)


def lenslet_slopes(band, blocks, step_x, step_y, rows, cols, ext, interpret=False):
    steps, layers, stars = step_x.shape
    padded = ext - 2 * HALO
    main = rows // LANES
    tiles = GROUP * main + (1 if rows % LANES else 0)
    groups = stars // GROUP
    smem = pl.BlockSpec(memory_space=pltpu.SMEM)
    vmem = pl.BlockSpec(memory_space=pltpu.VMEM)
    out = pl.pallas_call(
        functools.partial(lenslet_kernel, layers, stars, rows, padded, cols),
        out_shape=jax.ShapeDtypeStruct((steps * groups, 2, tiles * SUBS, LANES), jnp.float32),
        in_specs=[smem] * 3 + [vmem],
        out_specs=vmem,
        scratch_shapes=[
            pltpu.VMEM((layers, band.shape[2] // LANES, ext + NEW_COLS, LANES), jnp.float32),
            pltpu.VMEM((2 * padded, 3 * padded), jnp.bfloat16),
            pltpu.VMEM((padded, 2 * padded), jnp.bfloat16),
            pltpu.VMEM((2 * LANES, 2 * LANES), jnp.bfloat16),
            pltpu.VMEM((2 * LANES, LANES), jnp.bfloat16),
            pltpu.VMEM((SUBS, 2 * padded), jnp.bfloat16),
            pltpu.VMEM((2 * LANES, LANES), jnp.bfloat16),
        ],
        compiler_params=pltpu.CompilerParams(vmem_limit_bytes=40 * 1024 * 1024),
        interpret=interpret,
    )(blocks.reshape(-1), step_x.reshape(-1), step_y.reshape(-1), band)
    out = out.reshape(steps, groups, 2, tiles, SUBS, LANES)[:, :, :, :, : cols // PIX]
    found = []
    if main:
        part = out[:, :, :, : GROUP * main, :, : LANES // PIX]
        part = part.reshape(steps, groups, 2, GROUP, main, cols // PIX, LANES // PIX)
        part = jnp.transpose(part, (0, 1, 3, 5, 2, 4, 6))
        found.append(part.reshape(steps, stars, cols // PIX, 2, main * LANES // PIX))
    rem = rows % LANES // PIX
    if rem:
        part = out[:, :, :, GROUP * main, :, : GROUP * rem]
        part = part.reshape(steps, groups, 2, cols // PIX, GROUP, rem)
        part = jnp.transpose(part, (0, 1, 4, 3, 2, 5))
        found.append(part.reshape(steps, stars, cols // PIX, 2, rem))
    return jnp.concatenate(found, axis=4) if len(found) > 1 else found[0]


def sum_kernel(
    part_ref, out_ref, by_layer, by_sub, mine,
    send_1, recv_1, send_2, recv_2, send_3, recv_3, send_4, recv_4,
):
    layers, subs = part_ref.shape[0], part_ref.shape[1]
    me_l = lax.axis_index("layer")
    me_s = lax.axis_index("sub")
    mesh_id = pl.DeviceIdType.MESH
    layer_peers = [lax.rem(me_l + j, layers) for j in range(1, layers)]
    sub_peers = [lax.rem(me_s + j, subs) for j in range(1, subs)]

    barrier = pltpu.get_barrier_semaphore()
    for p in layer_peers:
        pl.semaphore_signal(barrier, inc=1, device_id=(p, me_s), device_id_type=mesh_id)
    for q in sub_peers:
        pl.semaphore_signal(barrier, inc=1, device_id=(me_l, q), device_id_type=mesh_id)
    pl.semaphore_wait(barrier, layers + subs - 2)

    def push(src, dst, send, recv, j, target):
        copy = pltpu.make_async_remote_copy(
            src_ref=src, dst_ref=dst, send_sem=send.at[j], recv_sem=recv.at[j],
            device_id=target, device_id_type=mesh_id,
        )
        copy.start()
        return copy

    copies = [
        push(part_ref.at[p], by_layer.at[j], send_1, recv_1, j, (p, me_s))
        for j, p in enumerate(layer_peers)
    ]
    for copy in copies:
        copy.wait()
    total = part_ref[me_l]
    for j in range(layers - 1):
        total = total + by_layer[j]
    mine[...] = total

    copies = [
        push(mine.at[q], by_sub.at[j], send_2, recv_2, j, (me_l, q))
        for j, q in enumerate(sub_peers)
    ]
    for copy in copies:
        copy.wait()
    total = mine[me_s]
    for j in range(subs - 1):
        total = total + by_sub[j]
    out_ref[me_l, me_s] = total

    own = out_ref.at[me_l, me_s]
    copies = [
        push(own, own, send_3, recv_3, j, (me_l, q)) for j, q in enumerate(sub_peers)
    ]
    for copy in copies:
        copy.wait()
    own = out_ref.at[me_l]
    copies = [
        push(own, own, send_4, recv_4, j, (p, me_s)) for j, p in enumerate(layer_peers)
    ]
    for copy in copies:
        copy.wait()


def summed_everywhere(part):
    layers = lax.axis_size("layer")
    subs = lax.axis_size("sub")
    lines = part.size // LANES
    chunk = -(-lines // (layers * subs * 8)) * 8
    padded = jnp.pad(part.reshape(lines, LANES), ((0, layers * subs * chunk - lines), (0, 0)))
    padded = padded.reshape(layers, subs, chunk, LANES)
    vmem = pl.BlockSpec(memory_space=pltpu.VMEM)
    dma = pltpu.SemaphoreType.DMA
    total = pl.pallas_call(
        sum_kernel,
        out_shape=jax.ShapeDtypeStruct(padded.shape, jnp.float32),
        in_specs=[vmem],
        out_specs=vmem,
        scratch_shapes=[
            pltpu.VMEM((layers - 1, subs, chunk, LANES), jnp.float32),
            pltpu.VMEM((subs - 1, chunk, LANES), jnp.float32),
            pltpu.VMEM((subs, chunk, LANES), jnp.float32),
            dma((layers - 1,)), dma((layers - 1,)),
            dma((subs - 1,)), dma((subs - 1,)),
            dma((subs - 1,)), dma((subs - 1,)),
            dma((layers - 1,)), dma((layers - 1,)),
        ],
        compiler_params=pltpu.CompilerParams(
            collective_id=0, has_side_effects=True, vmem_limit_bytes=32 * 1024 * 1024
        ),
    )(padded)
    return total.reshape(-1, LANES)[:lines].reshape(part.shape)


def exchange_kernel(sent_ref, got_ref, send, recv):
    layers = sent_ref.shape[0]
    rims = sent_ref.shape[1] - 2 * HALO
    me_l = lax.axis_index("layer")
    me_s = lax.axis_index("sub")
    subs = lax.axis_size("sub")
    right = lax.rem(me_s + 1, subs)
    left = lax.rem(me_s + subs - 1, subs)
    mesh_id = pl.DeviceIdType.MESH
    peers = [lax.rem(me_l + j, layers) for j in range(layers)]

    barrier = pltpu.get_barrier_semaphore()
    for p in peers[1:]:
        pl.semaphore_signal(barrier, inc=1, device_id=(p, me_s), device_id_type=mesh_id)
    for p in peers:
        for side in (right, left):
            pl.semaphore_signal(barrier, inc=1, device_id=(p, side), device_id_type=mesh_id)
    pl.semaphore_wait(barrier, 3 * layers - 1)

    copies = []

    def push(p, side, start, size):
        at = pl.ds(start, size)
        copy = pltpu.make_async_remote_copy(
            src_ref=sent_ref.at[p, at], dst_ref=got_ref.at[me_l, at],
            send_sem=send.at[len(copies)], recv_sem=recv.at[len(copies)],
            device_id=(p, side), device_id_type=mesh_id,
        )
        copy.start()
        copies.append(copy)

    for p in peers[1:]:
        push(p, me_s, 0, rims)
    for p in peers:
        push(p, right, rims, HALO)
        push(p, left, rims + HALO, HALO)
    got_ref[me_l, 0:rims] = sent_ref[me_l, 0:rims]
    for copy in copies:
        copy.wait()


def exchanged(sent):
    vmem = pl.BlockSpec(memory_space=pltpu.VMEM)
    count = 3 * sent.shape[0] - 1
    return pl.pallas_call(
        exchange_kernel,
        out_shape=jax.ShapeDtypeStruct(sent.shape, sent.dtype),
        in_specs=[vmem],
        out_specs=vmem,
        scratch_shapes=[pltpu.SemaphoreType.DMA((count,)), pltpu.SemaphoreType.DMA((count,))],
        compiler_params=pltpu.CompilerParams(
            collective_id=1, has_side_effects=True, vmem_limit_bytes=32 * 1024 * 1024
        ),
    )(sent)


def local(screens, new_columns, col_block, shift_x, shift_y, valid, recon):
    width = screens.shape[3]
    steps, _, stars = shift_x.shape
    count = lax.axis_size("layer")
    owner = lax.axis_index("sub")
    subs = lax.axis_size("sub")
    rows = valid.shape[0] * PIX
    cols = -(-width // 16) * 16
    ext = cols + 2 * HALO
    lanes = -(-(rows + 2 * HALO) // LANES) * LANES

    band = screens[0, PUP_TURN - 1 : PUP_TURN + 2, ROW0 - HALO : ROW0 + PUP + HALO, :]
    band = jnp.transpose(band, (0, 2, 1))
    tail = jnp.where(owner == subs - 1, band[0, width - HALO :], band[1, width - HALO :])
    head = jnp.where(owner == 0, band[2, :HALO], band[1, :HALO])
    fresh = jnp.transpose(new_columns[:, 0, ROW0 - HALO : ROW0 + PUP + HALO, :], (0, 2, 1))
    fresh = fresh.reshape(steps * NEW_COLS, PUP + 2 * HALO)
    strip = jnp.concatenate([band[1], fresh, jnp.zeros((8, band.shape[2])), tail, head], axis=0)
    plan = jnp.concatenate(
        [col_block.reshape(-1), shift_x.reshape(-1), shift_y.reshape(-1)]
    ).astype(jnp.float32)
    lines = -(-plan.shape[0] // lanes)
    plan = jnp.pad(plan, (0, 8 * lanes - plan.shape[0])).reshape(8, lanes)

    last = width + steps * NEW_COLS

    def share(i):
        cut = strip[:, i * rows : i * rows + rows + 2 * HALO]
        cut = jnp.pad(cut, ((0, 0), (0, lanes - cut.shape[1])))
        return cut.at[last : last + 8].set(plan)

    got = exchanged(jnp.stack([share(i) for i in range(count)]))

    plans = got[:, last : last + lines].reshape(count, -1).astype(jnp.int32)
    blocks = plans[:, :steps].T
    step_x = plans[:, steps : steps + steps * stars].reshape(count, steps, stars)
    step_y = plans[:, steps + steps * stars : steps + 2 * steps * stars]
    step_x = jnp.transpose(step_x, (1, 0, 2))
    step_y = jnp.transpose(step_y.reshape(count, steps, stars), (1, 0, 2))
    spot = blocks - PUP_TURN * PUP // NEW_COLS - owner * (width // NEW_COLS) + HALO // NEW_COLS
    inside = (spot >= 0) & (spot < (width + 2 * HALO) // NEW_COLS)
    spot = jnp.where(inside, spot, ext // NEW_COLS)

    slopes = lenslet_slopes(got, spot, step_x, step_y, rows, width, ext)
    slopes = slopes * valid.T.astype(jnp.float32)[None, None, :, None, :]
    flat = jnp.transpose(slopes, (0, 1, 4, 2, 3)).astype(jnp.bfloat16).reshape(steps, -1)
    matrix = jnp.transpose(recon, (0, 2, 3, 1, 4)).reshape(-1, ACTS)
    part = jnp.dot(flat, matrix, preferred_element_type=jnp.float32)
    commands = summed_everywhere(part)
    return (jnp.transpose(slopes, (0, 1, 3, 4, 2)), commands)


def solution(mesh):
    return jax.shard_map(
        local,
        mesh=mesh,
        in_specs=(
            P("layer", None, None, "sub"),
            P(None, "layer", None, None),
            P(None, "layer"),
            P(None, "layer", None),
            P(None, "layer", None),
            P("layer", "sub"),
            P(None, None, "layer", "sub", None),
        ),
        out_specs=(P(None, None, None, "layer", "sub"), P()),
        check_vma=False,
    )
```

```python
import functools
import math

import jax
import jax.numpy as jnp
import numpy as np
from jax import lax
from jax.experimental import pallas as pl
from jax.experimental.pallas import tpu as pltpu
from jax.sharding import PartitionSpec as P

FFT_LEN = 16
ACTS = 5376
HALO = 40
NEW_COLS = 8
PUP = 640
PUP_TURN = 3
ROW0 = 704
PIX = 8
LANES = 128
GROUP = 3
SUBS = 16


def sin_cos(x):
    k = jnp.floor(x * np.float32(2.0 / math.pi) + np.float32(0.5))
    r = x - k * np.float32(1.5703125)
    r = r - k * np.float32(4.837512969970703125e-4)
    r = r - k * np.float32(7.54978995489188216e-8)
    z = r * r
    sr = (np.float32(-1.9515295891e-4) * z + np.float32(8.3321608736e-3)) * z
    sr = r + r * z * (sr + np.float32(-1.6666654611e-1))
    cr = (np.float32(2.443315711809948e-5) * z + np.float32(-1.388731625493765e-3)) * z
    cr = z * z * (cr + np.float32(4.166664568298827e-2))
    cr = cr - np.float32(0.5) * z + np.float32(1.0)
    q = k.astype(jnp.int32)
    swap = (q & 1) == 1
    s = jnp.where(swap, cr, sr)
    c = jnp.where(swap, sr, cr)
    s = jnp.where((q & 2) == 2, -s, s)
    c = jnp.where(((q + 1) & 2) == 2, -c, c)
    return s, c


def split(x):
    high = x.astype(jnp.bfloat16)
    low = (x - high.astype(jnp.float32)).astype(jnp.bfloat16)
    return high, low


def lattice(shape):
    return tuple(lax.broadcasted_iota(jnp.int32, shape, axis) for axis in (0, 1))


def odd_form(row, col):
    gap = row - col
    value = jnp.zeros(row.shape, jnp.float32)
    for d in range(1, PIX):
        weight = np.float32(-((-1.0) ** d) / math.tan(math.pi * d / FFT_LEN))
        value = jnp.where(gap == d, weight, jnp.where(gap == -d, -weight, value))
    return jnp.where((row >> 3) == (col >> 3), value, 0.0)


def even_form(row, col):
    value = jnp.where(((row + col) & 1) == 1, np.float32(0.5), np.float32(-0.5))
    return jnp.where((row >> 3) == (col >> 3), value, 0.0)


def fill_constants(cols, used, left_c, left_s, right_c, right_e, sum_l, sum_r):
    row, col = lattice((cols, 3 * cols))
    third = col >= 2 * cols
    inner = col - jnp.where(third, 2 * cols, jnp.where(col >= cols, cols, 0))
    value = odd_form(row, inner)
    high = value.astype(jnp.bfloat16).astype(jnp.float32)
    left_c[0:cols, :] = jnp.where(third, value - high, high).astype(jnp.bfloat16)
    left_c[cols:, :] = jnp.where(third, 0.0, even_form(row, inner)).astype(jnp.bfloat16)
    row, col = lattice((cols, 2 * cols))
    inner = col - jnp.where(col >= cols, cols, 0)
    left_s[...] = even_form(row, inner).astype(jnp.bfloat16)
    row, col = lattice((2 * LANES, 2 * LANES))
    value = odd_form(col & (LANES - 1), row & (LANES - 1))
    high = value.astype(jnp.bfloat16).astype(jnp.float32)
    low = jnp.where(row < LANES, value - high, 0.0)
    right_c[...] = jnp.where(col < LANES, high, low).astype(jnp.bfloat16)
    row, col = lattice((2 * LANES, LANES))
    row = row & (LANES - 1)
    right_e[...] = even_form(row, col).astype(jnp.bfloat16)
    sum_r[...] = jnp.where((row >> 3) == col, 1.0, 0.0).astype(jnp.bfloat16)
    row, col = lattice((SUBS, 2 * cols))
    inner = col - jnp.where(col >= cols, cols, 0)
    inside = ((inner >> 3) == row) & (inner < used)
    sum_l[...] = jnp.where(inside, 1.0, 0.0).astype(jnp.bfloat16)


def mm(a, b):
    return jnp.dot(a, b, preferred_element_type=jnp.float32)


def lenslet_kernel(
    layers, stars, rows, cols, used,
    blk_ref, sx_ref, sy_ref, band_ref, out_ref, screen_ref,
    left_c_ref, left_s_ref, right_c_ref, right_e_ref, sum_l_ref, sum_r_ref,
):
    main = rows // LANES
    rem = rows % LANES
    tiles = band_ref.shape[2] // LANES
    groups = stars // GROUP
    lane = lax.broadcasted_iota(jnp.int32, (cols, LANES), 1)

    fill_constants(
        cols, used, left_c_ref, left_s_ref, right_c_ref, right_e_ref, sum_l_ref, sum_r_ref
    )
    rims = band_ref.shape[1] - 2 * HALO
    for l in range(layers):
        for j in range(tiles):
            cut = slice(j * LANES, (j + 1) * LANES)
            screen_ref[l, j, 0:HALO, :] = band_ref[l, rims : rims + HALO, cut]
            screen_ref[l, j, HALO : HALO + used, :] = band_ref[l, 0:used, cut]
            screen_ref[l, j, HALO + used : 2 * HALO + used, :] = band_ref[l, rims + HALO :, cut]
            if cols > used:
                screen_ref[l, j, 2 * HALO + used : 2 * HALO + cols, :] = jnp.zeros(
                    (cols - used, LANES), jnp.float32
                )

    def body(i, carry):
        t = i // groups
        h = i % groups
        for l in range(layers):
            start = pl.multiple_of(blk_ref[t * layers + l] * NEW_COLS, NEW_COLS)
            row = pl.multiple_of(used + t * NEW_COLS, NEW_COLS)
            for j in range(tiles):
                screen_ref[l, j, pl.ds(start, NEW_COLS), :] = band_ref[
                    l, pl.ds(row, NEW_COLS), j * LANES : (j + 1) * LANES
                ]
        parts = []
        tail = None
        for k in range(GROUP):
            sums = [None] * (main + 1)
            for l in range(layers):
                at = (t * layers + l) * stars + h * GROUP + k
                dx = sx_ref[at] + HALO
                dy = sy_ref[at] + HALO
                turn = lax.rem(LANES - dy, LANES)
                rolled = [
                    pltpu.roll(screen_ref[l, j, pl.ds(dx, cols), :], turn, 1)
                    for j in range(main + 1)
                ]
                keep = lane < LANES - dy
                for j in range(main + 1):
                    if j < main:
                        piece = jnp.where(keep, rolled[j], rolled[j + 1])
                    else:
                        piece = rolled[j]
                    sums[j] = piece if sums[j] is None else sums[j] + piece
            parts.extend(sums[:main])
            if rem:
                moved = sums[main] if k == 0 else pltpu.roll(sums[main], k * rem, 1)
                tail = moved if tail is None else jnp.where(lane < k * rem, tail, moved)
        if rem:
            parts.append(tail)
        phase = jnp.concatenate(parts, axis=1)
        s, c = sin_cos(phase)
        ch, cl = split(c)
        sh, sl = split(s)
        from_c = mm(left_c_ref[...], jnp.concatenate([ch, cl, ch], axis=0))
        from_s = mm(left_s_ref[...], jnp.concatenate([sh, sl], axis=0))
        along_x = s * (from_c[0:cols] + from_s) + c * from_c[cols:]
        power = c * c + s * s
        along_y = []
        for j in range(len(parts)):
            cut = slice(j * LANES, (j + 1) * LANES)
            pair_c = jnp.concatenate([ch[:, cut], cl[:, cut]], axis=1)
            pair_s = jnp.concatenate([sh[:, cut], sl[:, cut]], axis=1)
            odd = mm(pair_c, right_c_ref[...])
            odd = odd[:, :LANES] + odd[:, LANES:]
            along_y.append(
                s[:, cut] * (odd + mm(pair_s, right_e_ref[...]))
                + c[:, cut] * mm(pair_c, right_e_ref[...])
            )
        every = jnp.concatenate([along_x] + along_y + [power], axis=1)
        high, low = split(every)
        every = mm(sum_l_ref[...], jnp.concatenate([high, low], axis=0))
        count = 3 * len(parts)
        every = jnp.concatenate(
            [every[:, j * LANES : (j + 1) * LANES] for j in range(count)], axis=0
        )
        high, low = split(every)
        every = mm(jnp.concatenate([high, low], axis=1), sum_r_ref[...])
        size = len(parts) * SUBS
        total = every[2 * size :]
        out_ref[i, 0] = every[:size] / total
        out_ref[i, 1] = every[size : 2 * size] / total
        return carry

    lax.fori_loop(0, blk_ref.shape[0] // layers * groups, body, 0, unroll=2)


def lenslet_slopes(band, blocks, step_x, step_y, rows, cols, ext, interpret=False):
    steps, layers, stars = step_x.shape
    padded = ext - 2 * HALO
    main = rows // LANES
    tiles = GROUP * main + (1 if rows % LANES else 0)
    groups = stars // GROUP
    smem = pl.BlockSpec(memory_space=pltpu.SMEM)
    vmem = pl.BlockSpec(memory_space=pltpu.VMEM)
    out = pl.pallas_call(
        functools.partial(lenslet_kernel, layers, stars, rows, padded, cols),
        out_shape=jax.ShapeDtypeStruct((steps * groups, 2, tiles * SUBS, LANES), jnp.float32),
        in_specs=[smem] * 3 + [vmem],
        out_specs=vmem,
        scratch_shapes=[
            pltpu.VMEM((layers, band.shape[2] // LANES, ext + NEW_COLS, LANES), jnp.float32),
            pltpu.VMEM((2 * padded, 3 * padded), jnp.bfloat16),
            pltpu.VMEM((padded, 2 * padded), jnp.bfloat16),
            pltpu.VMEM((2 * LANES, 2 * LANES), jnp.bfloat16),
            pltpu.VMEM((2 * LANES, LANES), jnp.bfloat16),
            pltpu.VMEM((SUBS, 2 * padded), jnp.bfloat16),
            pltpu.VMEM((2 * LANES, LANES), jnp.bfloat16),
        ],
        compiler_params=pltpu.CompilerParams(vmem_limit_bytes=40 * 1024 * 1024),
        interpret=interpret,
    )(blocks.reshape(-1), step_x.reshape(-1), step_y.reshape(-1), band)
    out = out.reshape(steps, groups, 2, tiles, SUBS, LANES)[:, :, :, :, : cols // PIX]
    found = []
    if main:
        part = out[:, :, :, : GROUP * main, :, : LANES // PIX]
        part = part.reshape(steps, groups, 2, GROUP, main, cols // PIX, LANES // PIX)
        part = jnp.transpose(part, (0, 1, 3, 5, 2, 4, 6))
        found.append(part.reshape(steps, stars, cols // PIX, 2, main * LANES // PIX))
    rem = rows % LANES // PIX
    if rem:
        part = out[:, :, :, GROUP * main, :, : GROUP * rem]
        part = part.reshape(steps, groups, 2, cols // PIX, GROUP, rem)
        part = jnp.transpose(part, (0, 1, 4, 3, 2, 5))
        found.append(part.reshape(steps, stars, cols // PIX, 2, rem))
    return jnp.concatenate(found, axis=4) if len(found) > 1 else found[0]


def sum_kernel(
    part_ref, out_ref, by_layer, by_sub, mine,
    send_1, recv_1, send_2, recv_2, send_3, recv_3, send_4, recv_4,
):
    layers, subs = part_ref.shape[0], part_ref.shape[1]
    me_l = lax.axis_index("layer")
    me_s = lax.axis_index("sub")
    mesh_id = pl.DeviceIdType.MESH
    layer_peers = [lax.rem(me_l + j, layers) for j in range(1, layers)]
    sub_peers = [lax.rem(me_s + j, subs) for j in range(1, subs)]

    barrier = pltpu.get_barrier_semaphore()
    for p in layer_peers:
        pl.semaphore_signal(barrier, inc=1, device_id=(p, me_s), device_id_type=mesh_id)
    for q in sub_peers:
        pl.semaphore_signal(barrier, inc=1, device_id=(me_l, q), device_id_type=mesh_id)
    pl.semaphore_wait(barrier, layers + subs - 2)

    def push(src, dst, send, recv, j, target):
        copy = pltpu.make_async_remote_copy(
            src_ref=src, dst_ref=dst, send_sem=send.at[j], recv_sem=recv.at[j],
            device_id=target, device_id_type=mesh_id,
        )
        copy.start()
        return copy

    copies = [
        push(part_ref.at[p], by_layer.at[j], send_1, recv_1, j, (p, me_s))
        for j, p in enumerate(layer_peers)
    ]
    for copy in copies:
        copy.wait()
    total = part_ref[me_l]
    for j in range(layers - 1):
        total = total + by_layer[j]
    mine[...] = total

    copies = [
        push(mine.at[q], by_sub.at[j], send_2, recv_2, j, (me_l, q))
        for j, q in enumerate(sub_peers)
    ]
    for copy in copies:
        copy.wait()
    total = mine[me_s]
    for j in range(subs - 1):
        total = total + by_sub[j]
    out_ref[me_l, me_s] = total

    own = out_ref.at[me_l, me_s]
    copies = [
        push(own, own, send_3, recv_3, j, (me_l, q)) for j, q in enumerate(sub_peers)
    ]
    for j in range(subs):
        if j:
            copies[j - 1].wait()
        own = out_ref.at[me_l, lax.rem(me_s + subs - j, subs)]
        copies.extend(
            push(own, own, send_4, recv_4, j * (layers - 1) + i, (p, me_s))
            for i, p in enumerate(layer_peers)
        )
    for copy in copies[subs - 1 :]:
        copy.wait()


def summed_everywhere(part):
    layers = lax.axis_size("layer")
    subs = lax.axis_size("sub")
    lines = part.size // LANES
    chunk = -(-lines // (layers * subs * 8)) * 8
    padded = jnp.pad(part.reshape(lines, LANES), ((0, layers * subs * chunk - lines), (0, 0)))
    padded = padded.reshape(layers, subs, chunk, LANES)
    vmem = pl.BlockSpec(memory_space=pltpu.VMEM)
    dma = pltpu.SemaphoreType.DMA
    total = pl.pallas_call(
        sum_kernel,
        out_shape=jax.ShapeDtypeStruct(padded.shape, jnp.float32),
        in_specs=[vmem],
        out_specs=vmem,
        scratch_shapes=[
            pltpu.VMEM((layers - 1, subs, chunk, LANES), jnp.float32),
            pltpu.VMEM((subs - 1, chunk, LANES), jnp.float32),
            pltpu.VMEM((subs, chunk, LANES), jnp.float32),
            dma((layers - 1,)), dma((layers - 1,)),
            dma((subs - 1,)), dma((subs - 1,)),
            dma((subs - 1,)), dma((subs - 1,)),
            dma((subs * (layers - 1),)), dma((subs * (layers - 1),)),
        ],
        compiler_params=pltpu.CompilerParams(
            collective_id=0, has_side_effects=True, vmem_limit_bytes=32 * 1024 * 1024
        ),
    )(padded)
    return total.reshape(-1, LANES)[:lines].reshape(part.shape)


def exchange_kernel(sent_ref, got_ref, send, recv):
    layers = sent_ref.shape[0]
    rims = sent_ref.shape[1] - 2 * HALO
    me_l = lax.axis_index("layer")
    me_s = lax.axis_index("sub")
    subs = lax.axis_size("sub")
    right = lax.rem(me_s + 1, subs)
    left = lax.rem(me_s + subs - 1, subs)
    mesh_id = pl.DeviceIdType.MESH
    peers = [lax.rem(me_l + j, layers) for j in range(layers)]

    barrier = pltpu.get_barrier_semaphore()
    for p in peers[1:]:
        pl.semaphore_signal(barrier, inc=1, device_id=(p, me_s), device_id_type=mesh_id)
    for p in peers:
        for side in (right, left):
            pl.semaphore_signal(barrier, inc=1, device_id=(p, side), device_id_type=mesh_id)
    pl.semaphore_wait(barrier, 3 * layers - 1)

    copies = []

    def push(p, side, start, size):
        at = pl.ds(start, size)
        copy = pltpu.make_async_remote_copy(
            src_ref=sent_ref.at[p, at], dst_ref=got_ref.at[me_l, at],
            send_sem=send.at[len(copies)], recv_sem=recv.at[len(copies)],
            device_id=(p, side), device_id_type=mesh_id,
        )
        copy.start()
        copies.append(copy)

    for p in peers[1:]:
        push(p, me_s, 0, rims)
    for p in peers:
        push(p, right, rims, HALO)
        push(p, left, rims + HALO, HALO)
    got_ref[me_l, 0:rims] = sent_ref[me_l, 0:rims]
    for copy in copies:
        copy.wait()


def exchanged(sent):
    vmem = pl.BlockSpec(memory_space=pltpu.VMEM)
    count = 3 * sent.shape[0] - 1
    return pl.pallas_call(
        exchange_kernel,
        out_shape=jax.ShapeDtypeStruct(sent.shape, sent.dtype),
        in_specs=[vmem],
        out_specs=vmem,
        scratch_shapes=[pltpu.SemaphoreType.DMA((count,)), pltpu.SemaphoreType.DMA((count,))],
        compiler_params=pltpu.CompilerParams(
            collective_id=1, has_side_effects=True, vmem_limit_bytes=32 * 1024 * 1024
        ),
    )(sent)


def local(screens, new_columns, col_block, shift_x, shift_y, valid, recon):
    width = screens.shape[3]
    steps, _, stars = shift_x.shape
    count = lax.axis_size("layer")
    owner = lax.axis_index("sub")
    subs = lax.axis_size("sub")
    rows = valid.shape[0] * PIX
    cols = -(-width // 16) * 16
    ext = cols + 2 * HALO
    lanes = -(-(rows + 2 * HALO) // LANES) * LANES

    band = screens[0, PUP_TURN - 1 : PUP_TURN + 2, ROW0 - HALO : ROW0 + PUP + HALO, :]
    band = jnp.transpose(band, (0, 2, 1))
    tail = jnp.where(owner == subs - 1, band[0, width - HALO :], band[1, width - HALO :])
    head = jnp.where(owner == 0, band[2, :HALO], band[1, :HALO])
    fresh = jnp.transpose(new_columns[:, 0, ROW0 - HALO : ROW0 + PUP + HALO, :], (0, 2, 1))
    fresh = fresh.reshape(steps * NEW_COLS, PUP + 2 * HALO)
    strip = jnp.concatenate([band[1], fresh, jnp.zeros((8, band.shape[2])), tail, head], axis=0)
    plan = jnp.concatenate(
        [col_block.reshape(-1), shift_x.reshape(-1), shift_y.reshape(-1)]
    ).astype(jnp.float32)
    lines = -(-plan.shape[0] // lanes)
    plan = jnp.pad(plan, (0, 8 * lanes - plan.shape[0])).reshape(8, lanes)

    last = width + steps * NEW_COLS

    def share(i):
        cut = strip[:, i * rows : i * rows + rows + 2 * HALO]
        cut = jnp.pad(cut, ((0, 0), (0, lanes - cut.shape[1])))
        return cut.at[last : last + 8].set(plan)

    got = exchanged(jnp.stack([share(i) for i in range(count)]))

    plans = got[:, last : last + lines].reshape(count, -1).astype(jnp.int32)
    blocks = plans[:, :steps].T
    step_x = plans[:, steps : steps + steps * stars].reshape(count, steps, stars)
    step_y = plans[:, steps + steps * stars : steps + 2 * steps * stars]
    step_x = jnp.transpose(step_x, (1, 0, 2))
    step_y = jnp.transpose(step_y.reshape(count, steps, stars), (1, 0, 2))
    spot = blocks - PUP_TURN * PUP // NEW_COLS - owner * (width // NEW_COLS) + HALO // NEW_COLS
    inside = (spot >= 0) & (spot < (width + 2 * HALO) // NEW_COLS)
    spot = jnp.where(inside, spot, ext // NEW_COLS)

    slopes = lenslet_slopes(got, spot, step_x, step_y, rows, width, ext)
    slopes = slopes * valid.T.astype(jnp.float32)[None, None, :, None, :]
    flat = jnp.transpose(slopes, (0, 1, 4, 2, 3)).astype(jnp.bfloat16).reshape(steps, -1)
    matrix = jnp.transpose(recon, (0, 2, 3, 1, 4)).reshape(-1, ACTS)
    part = jnp.dot(flat, matrix, preferred_element_type=jnp.float32)
    commands = summed_everywhere(part)
    return (jnp.transpose(slopes, (0, 1, 3, 4, 2)), commands)


def solution(mesh):
    return jax.shard_map(
        local,
        mesh=mesh,
        in_specs=(
            P("layer", None, None, "sub"),
            P(None, "layer", None, None),
            P(None, "layer"),
            P(None, "layer", None),
            P(None, "layer", None),
            P("layer", "sub"),
            P(None, None, "layer", "sub", None),
        ),
        out_specs=(P(None, None, None, "layer", "sub"), P()),
        check_vma=False,
    )
```
